32 devices in a mesh: patch: 8 (over y, x, core), ulysses: 4 (over z).
Axes of the slice: x: 2, y: 2, z: 4, core: 2. Of those that a mesh axis runs over, the one named last changes fastest.
Arguments:
- fresh_queries: bfloat16 [512, 2048], P(('patch', 'ulysses')), may hold values from -12 to 12
- fresh_keys: bfloat16 [512, 2048], P(('patch', 'ulysses')), may hold values from -6 to 6
- fresh_values: bfloat16 [512, 2048], P(('patch', 'ulysses')), may hold values from -6 to 6
- outdated_keys: bfloat16 [512, 2048], P(None, 'ulysses'), may hold values from -6 to 6
- stale_values: bfloat16 [512, 2048], P(None, 'ulysses'), may hold values from -6 to 6
- key_codes: int32 [512, 2048], P('patch', 'ulysses'), may hold values from -127 to 127
- value_codes: int32 [512, 2048], P('patch', 'ulysses'), may hold values from -127 to 127
- key_code_scales: bfloat16 [64, 16], P('patch', 'ulysses'), may hold values from 0.0039978027 to 0.015991211
- value_scales: bfloat16 [64, 16], P('patch', 'ulysses'), may hold values from 0.0039978027 to 0.015991211
- out_weight: bfloat16 [2048, 3072], P('ulysses', 'patch'), may hold values from -1.5 to 1.5
Outputs:
- projected: bfloat16 [512, 3072], P(('patch', 'ulysses'))
The draws below stay inside these ranges and needn't reach their ends.
All inputs are finite; a program needn't handle non-finite values.
Results may differ from the reference program's by a relative error of at most 0.012.
The reference program's roundings to bfloat16 on the way count: a program that leaves them out, or rounds other values in their place, can miss the bound.
Values may be sent and summed in bfloat16 or wider, within the bound.
A program may use at most 64 MiB of HBM per device.

```python
import math
import jax
import jax.numpy as jnp
from jax import lax

D = 3072
HEADS = 16
HEAD_DIM = 128
BLOCK = 8
TOKENS = 512
N_PATCH = 8


def draw_fresh_queries(key, part):
    key = jax.random.fold_in(key, 11)
    filled = jnp.clip(2.0 * jax.random.normal(key, (TOKENS, HEADS * HEAD_DIM), jnp.float32), -12.0, 12.0)
    return filled.astype(jnp.bfloat16)


def draw_outdated_keys(key, part):
    key = jax.random.fold_in(key, 23)
    filled = jnp.clip(jax.random.normal(key, (TOKENS, HEADS * HEAD_DIM), jnp.float32), -6.0, 6.0)
    return filled.astype(jnp.bfloat16)


def place_ends(values, own_key, least, top_value):
    index_at = [jax.random.randint(jax.random.fold_in(own_key, axis), (), 0, length) for axis, length in enumerate(values.shape)]
    widest = values.shape.index(max(values.shape))
    next_to = index_at[:widest] + [(index_at[widest] + 1) % values.shape[widest]] + index_at[widest + 1:]
    return values.at[tuple(index_at)].set(least).at[tuple(next_to)].set(top_value)


def steps_of(key, extent, shards, least, high):
    level, own = 1.0, jax.random.fold_in(key, 6)
    for dim, shards_of in shards:
        draws = jnp.exp(jax.random.uniform(jax.random.fold_in(own, dim), (shards_of,), jnp.float32, least / len(shards), high / len(shards)))
        level = level * jnp.repeat(draws, extent[dim] // shards_of).reshape([-1 if axis == dim else 1 for axis in range(len(extent))])
    return level


def gaussian(key, dims, width, limit, pieces=(), dtype=jnp.bfloat16):
    level = steps_of(key, dims, pieces, -0.22, 0.18) if pieces else 1.0
    entries = jax.random.normal(key, dims, jnp.float32) * width * level
    return jnp.minimum(jnp.maximum(entries, -limit), limit).astype(dtype)


def setup_inputs(seed: int = 0) -> dict:
    splits = jax.random.split(jax.random.key(seed), 11)
    fresh_queries = draw_fresh_queries(jax.random.fold_in(splits[10], 71), 0)
    fresh_keys = gaussian(splits[1], (TOKENS, HEADS * HEAD_DIM), 1.0, 6.0, ((0, 32),))
    fresh_values = gaussian(splits[2], (TOKENS, HEADS * HEAD_DIM), 1.0, 6.0, ((0, 32),))
    outdated_keys = draw_outdated_keys(jax.random.fold_in(splits[10], 71), 0)
    stale_values = gaussian(splits[4], (TOKENS, HEADS * HEAD_DIM), 1.0, 6.0, ((1, 4),))
    key_codes = place_ends(jax.random.randint(splits[5], (TOKENS, HEADS * HEAD_DIM), -127, 128), jax.random.fold_in(splits[5], 1), -127, 127).astype(jnp.int32)
    value_codes = place_ends(jax.random.randint(splits[6], (TOKENS, HEADS * HEAD_DIM), -127, 128), jax.random.fold_in(splits[6], 1), -127, 127).astype(jnp.int32)
    key_code_scales = jnp.clip(jnp.exp(math.log(0.015991211) - 1.3862944 * jax.random.uniform(splits[7], (TOKENS // BLOCK, HEADS), jnp.float32) ** steps_of(splits[7], (TOKENS // BLOCK, HEADS), ((0, 8), (1, 4)), -0.2, 0.2)), 0.0039978027, 0.015991211).astype(jnp.bfloat16)
    value_scales = jnp.clip(jnp.exp(math.log(0.015991211) - 1.3862944 * jax.random.uniform(splits[8], (TOKENS // BLOCK, HEADS), jnp.float32) ** steps_of(splits[8], (TOKENS // BLOCK, HEADS), ((0, 8), (1, 4)), -0.2, 0.2)), 0.0039978027, 0.015991211).astype(jnp.bfloat16)
    out_weight = gaussian(splits[9], (HEADS * HEAD_DIM, D), (HEAD_DIM // 8) ** -0.5, 1.5, ((0, 4), (1, 8)))
    return {"fresh_queries": fresh_queries, "fresh_keys": fresh_keys, "fresh_values": fresh_values, "outdated_keys": outdated_keys, "stale_values": stale_values, "key_codes": key_codes, "value_codes": value_codes, "key_code_scales": key_code_scales, "value_scales": value_scales, "out_weight": out_weight}


def refresh_rows(stale, codes, scales):
    widened = jnp.repeat(jnp.repeat(scales.astype(jnp.float32), BLOCK, axis=0), HEAD_DIM, axis=1)
    return (stale.astype(jnp.float32) + widened * codes.astype(jnp.float32)).astype(jnp.bfloat16)

def reference(fresh_queries, fresh_keys, fresh_values, outdated_keys, stale_values, key_codes, value_codes, key_code_scales, value_scales, out_weight):
    patch_span = TOKENS // N_PATCH
    owner_patch = jnp.arange(TOKENS) // patch_span
    same_patch = owner_patch[:, None] == owner_patch[None, :]
    seen_keys = refresh_rows(outdated_keys, key_codes, key_code_scales)
    seen_values = refresh_rows(stale_values, value_codes, value_scales)
    scale_qk = 1.0 / math.sqrt(HEAD_DIM)

    def head_output(head_index):
        first_col = head_index * HEAD_DIM

        def columns(array):
            return lax.dynamic_slice_in_dim(array, first_col, HEAD_DIM, 1)
        query_cols = columns(fresh_queries)
        far_scores = jnp.dot(query_cols, columns(seen_keys).T, preferred_element_type=jnp.float32) * scale_qk
        far_scores = jnp.where(same_patch, -1e+30, far_scores)
        query_blocks = query_cols.reshape(N_PATCH, patch_span, HEAD_DIM).astype(jnp.float32)
        key_blocks = columns(fresh_keys).reshape(N_PATCH, patch_span, HEAD_DIM).astype(jnp.float32)
        near_scores = jnp.einsum('pqd,pkd->pqk', query_blocks, key_blocks) * scale_qk
        row_top = jnp.maximum(lax.optimization_barrier(jnp.max(far_scores, axis=1)), lax.optimization_barrier(jnp.max(near_scores, axis=2)).reshape(TOKENS))
        far_weights = jnp.exp(far_scores - row_top[:, None])
        near_weights = jnp.exp(near_scores - row_top.reshape(N_PATCH, patch_span)[:, :, None])
        totals = lax.optimization_barrier(jnp.sum(far_weights, axis=1)) + lax.optimization_barrier(jnp.sum(near_weights, axis=2)).reshape(TOKENS)
        far_part = jnp.dot(far_weights.astype(jnp.bfloat16), columns(seen_values), preferred_element_type=jnp.float32)
        value_blocks = columns(fresh_values).reshape(N_PATCH, patch_span, HEAD_DIM).astype(jnp.float32)
        near_part = jnp.einsum('pqk,pkd->pqd', near_weights.astype(jnp.bfloat16).astype(jnp.float32), value_blocks)
        numerator = far_part + near_part.reshape(TOKENS, HEAD_DIM)
        return (numerator / totals[:, None]).astype(jnp.bfloat16)
    per_head = lax.map(head_output, jnp.arange(HEADS).astype(jnp.int32))
    attended = jnp.transpose(per_head, (1, 0, 2)).reshape(TOKENS, HEADS * HEAD_DIM)
    return jnp.dot(attended, out_weight, preferred_element_type=jnp.float32).astype(jnp.bfloat16)
```

```python
import functools
import math

import jax
import jax.numpy as jnp
from jax import lax
from jax.experimental import pallas as pl
from jax.experimental.pallas import tpu as pltpu
from jax.sharding import PartitionSpec as P

HEAD_DIM = 128
BLOCK = 8
MESH = pl.DeviceIdType.MESH


def send(src, dst, send_sem, recv_sem, target, here):
    same = jnp.logical_and(target[0] == here[0], target[1] == here[1])

    @pl.when(same)
    def _():
        pltpu.make_async_copy(src, dst, recv_sem).start()

    @pl.when(jnp.logical_not(same))
    def _():
        pltpu.make_async_remote_copy(
            src, dst, send_sem, recv_sem, device_id=target, device_id_type=MESH
        ).start()


def finish_send(src, dst, send_sem, recv_sem, target, here):
    same = jnp.logical_and(target[0] == here[0], target[1] == here[1])

    @pl.when(jnp.logical_not(same))
    def _():
        pltpu.make_async_remote_copy(
            src, dst, send_sem, recv_sem, device_id=target, device_id_type=MESH
        ).wait_send()


def wait_bytes(buffer, sem):
    pltpu.make_async_copy(buffer, buffer, sem).wait()


def kernel(
    patches, groups,
    key_scales, value_scales,
    fresh_q, fresh_k, fresh_v, old_k, old_v, codes_k, codes_v, weight,
    out,
    fresh_in, old_in, codes_in, weight_in,
    fresh_out, fresh_got, seen_out, seen_got, key_work, value_work,
    attended_out, attended_got, terms_out, terms_got,
    load_sem, fresh_send, fresh_recv, seen_send, seen_recv,
    attended_send, attended_recv, terms_send, terms_recv,
):
    p = lax.axis_index("patch")
    u = lax.axis_index("ulysses")
    here = (p, u)
    rows = fresh_q.shape[0]
    span = rows * groups
    heads = fresh_q.shape[1] // HEAD_DIM
    local = heads // groups
    ranks = patches // local
    my_head = p // ranks
    my_rank = lax.rem(p, ranks)

    loads = [
        pltpu.make_async_copy(source, fresh_in.at[i], load_sem.at[i])
        for i, source in enumerate((fresh_q, fresh_k, fresh_v))
    ]
    first = pl.multiple_of(p * span, span)
    loads.append(pltpu.make_async_copy(old_k.at[pl.ds(first, span)], old_in.at[0], load_sem.at[3]))
    loads.append(pltpu.make_async_copy(old_v.at[pl.ds(first, span)], old_in.at[1], load_sem.at[4]))
    loads.append(pltpu.make_async_copy(codes_k, codes_in.at[0], load_sem.at[5]))
    loads.append(pltpu.make_async_copy(codes_v, codes_in.at[1], load_sem.at[6]))
    loads.append(pltpu.make_async_copy(weight, weight_in, load_sem.at[7]))
    for load in loads:
        load.start()

    barrier = pltpu.get_barrier_semaphore()
    devices = patches * groups

    def greet(i, carry):
        to_p, to_u = i // groups, lax.rem(i, groups)

        @pl.when(jnp.logical_not(jnp.logical_and(to_p == p, to_u == u)))
        def _():
            pl.semaphore_signal(barrier, inc=1, device_id=(to_p, to_u), device_id_type=MESH)

        return carry

    lax.fori_loop(0, devices, greet, 0)

    for load in loads[:3]:
        load.wait()
    for h in range(heads):
        for i in range(3):
            fresh_out[h, i] = fresh_in[i, :, h * HEAD_DIM:(h + 1) * HEAD_DIM]
    for load in loads[3:7]:
        load.wait()
    block_of = lax.broadcasted_iota(jnp.int32, (span, span // BLOCK), 0) // BLOCK
    pick = (block_of == lax.broadcasted_iota(jnp.int32, (span, span // BLOCK), 1)).astype(jnp.float32)
    for i, scales in enumerate((key_scales, value_scales)):
        wide = jnp.dot(
            pick, scales[...].astype(jnp.float32), preferred_element_type=jnp.float32
        )
        for l in range(local):
            cols = slice(l * HEAD_DIM, (l + 1) * HEAD_DIM)
            seen_out[l, i] = (
                old_in[i, :, cols].astype(jnp.float32)
                + wide[:, l:l + 1] * codes_in[i, :, cols].astype(jnp.float32)
            ).astype(jnp.bfloat16)

    pl.semaphore_wait(barrier, devices - 1)

    def fresh_args(i):
        h = lax.rem(u * local + local + i, heads)
        target = (lax.rem(h, local) * ranks + p // local, h // local)
        return (fresh_out.at[h], fresh_got.at[lax.rem(p, local), u],
                fresh_send.at[h], fresh_recv, target, here)

    def seen_args(i):
        to = lax.rem(p + 1 + i, patches)
        return (seen_out.at[to // ranks], seen_got.at[p], seen_send.at[to], seen_recv, (to, u), here)

    def start_fresh(i, carry):
        send(*fresh_args(i))
        return carry

    def start_seen(i, carry):
        send(*seen_args(i))
        return carry

    lax.fori_loop(0, heads, start_fresh, 0)
    lax.fori_loop(0, patches, start_seen, 0)
    wait_bytes(seen_got, seen_recv)
    for i in range(local):
        key_work[i] = seen_got[:, 0].reshape(patches * span, HEAD_DIM)
        value_work[i] = seen_got[:, 1].reshape(patches * span, HEAD_DIM)
    wait_bytes(fresh_got, fresh_recv)

    scale_qk = 1.0 / math.sqrt(HEAD_DIM)

    def attended_args(slot, patch, i):
        to = lax.rem(p + 1 + i, patches)
        return (attended_out.at[slot], attended_got.at[patch, my_head],
                attended_send.at[slot, to], attended_recv.at[patch], (to, u), here)

    def attend(slot):
        index = lax.rem(slot + u, local)
        patch = my_rank * local + index
        query = fresh_got[index, :, 0].reshape(span, HEAD_DIM)
        own = pl.ds(pl.multiple_of(patch * span, span), span)
        key_work[slot, own] = fresh_got[index, :, 1].reshape(span, HEAD_DIM)
        value_work[slot, own] = fresh_got[index, :, 2].reshape(span, HEAD_DIM)
        scores = lax.dot_general(
            query, key_work[slot], (((1,), (1,)), ((), ())), preferred_element_type=jnp.float32
        ) * scale_qk
        top = jnp.max(scores, axis=1, keepdims=True)
        weights = jnp.exp(scores - top)
        total = jnp.sum(weights, axis=1, keepdims=True)
        mixed = jnp.dot(
            weights.astype(jnp.bfloat16), value_work[slot], preferred_element_type=jnp.float32
        )
        attended_out[slot] = (mixed / total).astype(jnp.bfloat16)

        def start(i, carry):
            send(*attended_args(slot, patch, i))
            return carry

        lax.fori_loop(0, patches, start, 0)

    def terms_args(patch, i):
        to = lax.rem(u + 1 + i, groups)
        return (terms_out.at[patch, to], terms_got.at[u, p],
                terms_send.at[patch, to], terms_recv, (patch, to), here)

    def project(slot):
        index = lax.rem(slot + u, local)
        for r in range(ranks):
            patch = r * local + index
            wait_bytes(attended_got.at[patch], attended_recv.at[patch])
            gathered = jnp.concatenate([attended_got[patch, l] for l in range(local)], axis=1)
            terms = jnp.dot(gathered, weight_in[...], preferred_element_type=jnp.float32)
            terms_out[patch] = terms.astype(jnp.bfloat16).reshape(groups, rows, terms.shape[1])

            def start(i, carry):
                send(*terms_args(patch, i))
                return carry

            lax.fori_loop(0, groups, start, 0)

    for slot in range(local):
        attend(slot)
    loads[7].wait()
    for slot in range(local):
        project(slot)

    def end_fresh(i, carry):
        finish_send(*fresh_args(i))
        return carry

    def end_seen(i, carry):
        finish_send(*seen_args(i))
        return carry

    lax.fori_loop(0, heads, end_fresh, 0)
    lax.fori_loop(0, patches, end_seen, 0)
    for slot in range(local):
        patch = my_rank * local + lax.rem(slot + u, local)

        def end(i, carry):
            finish_send(*attended_args(slot, patch, i))
            return carry

        lax.fori_loop(0, patches, end, 0)

    def end_terms(i, carry):
        finish_send(*terms_args(i // groups, lax.rem(i, groups)))
        return carry

    wait_bytes(terms_got, terms_recv)
    columns = weight.shape[1]
    for q in range(patches):
        total = terms_got[0, q].astype(jnp.float32)
        for g in range(1, groups):
            total = total + terms_got[g, q].astype(jnp.float32)
        out[:, q * columns:(q + 1) * columns] = total.astype(jnp.bfloat16)
    lax.fori_loop(0, patches * groups, end_terms, 0)


def solution(mesh):
    patches, groups = mesh.shape["patch"], mesh.shape["ulysses"]

    def on_device(
        fresh_queries, fresh_keys, fresh_values, outdated_keys, stale_values,
        key_codes, value_codes, key_code_scales, value_scales, out_weight,
    ):
        rows, width = fresh_queries.shape
        span = rows * groups
        heads = width // HEAD_DIM
        local = heads // groups
        depth, columns = out_weight.shape
        bf16, f32 = jnp.bfloat16, jnp.float32
        vmem = pl.BlockSpec(memory_space=pltpu.VMEM)
        hbm = pl.BlockSpec(memory_space=pl.ANY)
        dma = pltpu.SemaphoreType.DMA
        return pl.pallas_call(
            functools.partial(kernel, patches, groups),
            out_shape=jax.ShapeDtypeStruct((rows, patches * columns), bf16),
            in_specs=[vmem] * 2 + [hbm] * 8,
            out_specs=vmem,
            scratch_shapes=[
                pltpu.VMEM((3, rows, width), bf16),
                pltpu.VMEM((2, span, depth), bf16),
                pltpu.VMEM((2, span, depth), jnp.int32),
                pltpu.VMEM((depth, columns), bf16),
                pltpu.VMEM((heads, 3, rows, HEAD_DIM), bf16),
                pltpu.VMEM((local, groups, 3, rows, HEAD_DIM), bf16),
                pltpu.VMEM((local, 2, span, HEAD_DIM), bf16),
                pltpu.VMEM((patches, 2, span, HEAD_DIM), bf16),
                pltpu.VMEM((local, patches * span, HEAD_DIM), bf16),
                pltpu.VMEM((local, patches * span, HEAD_DIM), bf16),
                pltpu.VMEM((local, span, HEAD_DIM), bf16),
                pltpu.VMEM((patches, local, span, HEAD_DIM), bf16),
                pltpu.VMEM((patches, groups, rows, columns), bf16),
                pltpu.VMEM((groups, patches, rows, columns), bf16),
                dma((8,)), dma((heads,)), dma, dma((patches,)), dma,
                dma((local, patches)), dma((patches,)), dma((patches, groups)), dma,
            ],
            compiler_params=pltpu.CompilerParams(
                collective_id=0, has_side_effects=True, vmem_limit_bytes=48 * 1024 * 1024
            ),
        )(
            key_code_scales, value_scales, fresh_queries, fresh_keys, fresh_values,
            outdated_keys, stale_values, key_codes, value_codes, out_weight,
        )

    return jax.shard_map(
        on_device,
        mesh=mesh,
        in_specs=(
            P(("patch", "ulysses"), None),
            P(("patch", "ulysses"), None),
            P(("patch", "ulysses"), None),
            P(None, "ulysses"),
            P(None, "ulysses"),
            P("patch", "ulysses"),
            P("patch", "ulysses"),
            P("patch", "ulysses"),
            P("patch", "ulysses"),
            P("ulysses", "patch"),
        ),
        out_specs=P(("patch", "ulysses"), None),
        check_vma=False,
    )
```

```python
import functools
import math

import jax
import jax.numpy as jnp
from jax import lax
from jax.experimental import pallas as pl
from jax.experimental.pallas import tpu as pltpu
from jax.sharding import PartitionSpec as P

HEAD_DIM = 128
BLOCK = 8
MESH = pl.DeviceIdType.MESH


def send(src, dst, send_sem, recv_sem, target, here):
    same = jnp.logical_and(target[0] == here[0], target[1] == here[1])

    @pl.when(same)
    def _():
        pltpu.make_async_copy(src, dst, recv_sem).start()

    @pl.when(jnp.logical_not(same))
    def _():
        pltpu.make_async_remote_copy(
            src, dst, send_sem, recv_sem, device_id=target, device_id_type=MESH
        ).start()


def finish_send(src, dst, send_sem, recv_sem, target, here):
    same = jnp.logical_and(target[0] == here[0], target[1] == here[1])

    @pl.when(jnp.logical_not(same))
    def _():
        pltpu.make_async_remote_copy(
            src, dst, send_sem, recv_sem, device_id=target, device_id_type=MESH
        ).wait_send()


def wait_bytes(buffer, sem):
    pltpu.make_async_copy(buffer, buffer, sem).wait()


def kernel(
    patches, groups,
    key_scales, value_scales,
    fresh_q, fresh_k, fresh_v, old_k, old_v, codes_k, codes_v, weight,
    out,
    fresh_in, old_in, codes_in, weight_in,
    fresh_out, fresh_got, seen_out, seen_got, key_work, value_work,
    attended_out, attended_got, terms_out, terms_got,
    load_sem, fresh_send, fresh_recv, seen_send, seen_recv,
    attended_send, attended_recv, terms_send, terms_recv,
):
    p = lax.axis_index("patch")
    u = lax.axis_index("ulysses")
    here = (p, u)
    rows = fresh_q.shape[0]
    span = rows * groups
    heads = fresh_q.shape[1] // HEAD_DIM
    local = heads // groups
    ranks = patches // local
    my_head = p // ranks
    my_rank = lax.rem(p, ranks)

    loads = [
        pltpu.make_async_copy(source, fresh_in.at[i], load_sem.at[i])
        for i, source in enumerate((fresh_q, fresh_k, fresh_v))
    ]
    first = pl.multiple_of(p * span, span)
    loads.append(pltpu.make_async_copy(old_k.at[pl.ds(first, span)], old_in.at[0], load_sem.at[3]))
    loads.append(pltpu.make_async_copy(old_v.at[pl.ds(first, span)], old_in.at[1], load_sem.at[4]))
    loads.append(pltpu.make_async_copy(codes_k, codes_in.at[0], load_sem.at[5]))
    loads.append(pltpu.make_async_copy(codes_v, codes_in.at[1], load_sem.at[6]))
    loads.append(pltpu.make_async_copy(weight, weight_in, load_sem.at[7]))
    for load in loads:
        load.start()

    barrier = pltpu.get_barrier_semaphore()
    devices = patches * groups

    def greet(i, carry):
        to_p, to_u = i // groups, lax.rem(i, groups)

        @pl.when(jnp.logical_not(jnp.logical_and(to_p == p, to_u == u)))
        def _():
            pl.semaphore_signal(barrier, inc=1, device_id=(to_p, to_u), device_id_type=MESH)

        return carry

    lax.fori_loop(0, devices, greet, 0)

    for load in loads[:3]:
        load.wait()
    for h in range(heads):
        for i in range(3):
            fresh_out[h, i] = fresh_in[i, :, h * HEAD_DIM:(h + 1) * HEAD_DIM]
    for load in loads[3:7]:
        load.wait()
    block_of = lax.broadcasted_iota(jnp.int32, (span, span // BLOCK), 0) // BLOCK
    pick = (block_of == lax.broadcasted_iota(jnp.int32, (span, span // BLOCK), 1)).astype(jnp.float32)
    for i, scales in enumerate((key_scales, value_scales)):
        wide = lax.dot_general(
            pick, scales[...].astype(jnp.float32), (((1,), (1,)), ((), ())),
            preferred_element_type=jnp.float32,
        )
        for l in range(local):
            cols = slice(l * HEAD_DIM, (l + 1) * HEAD_DIM)
            seen_out[l, i] = (
                old_in[i, :, cols].astype(jnp.float32)
                + wide[:, l:l + 1] * codes_in[i, :, cols].astype(jnp.float32)
            ).astype(jnp.bfloat16)

    pl.semaphore_wait(barrier, devices - 1)

    def fresh_args(i):
        h = lax.rem(u * local + local + i, heads)
        target = (lax.rem(h, local) * ranks + p // local, h // local)
        return (fresh_out.at[h], fresh_got.at[lax.rem(p, local), u],
                fresh_send.at[h], fresh_recv, target, here)

    def seen_args(i):
        to = lax.rem(p + 1 + i, patches)
        return (seen_out.at[to // ranks], seen_got.at[p], seen_send.at[to], seen_recv, (to, u), here)

    def start_fresh(i, carry):
        send(*fresh_args(i))
        return carry

    def start_seen(i, carry):
        send(*seen_args(i))
        return carry

    lax.fori_loop(0, heads, start_fresh, 0)
    lax.fori_loop(0, patches, start_seen, 0)
    wait_bytes(seen_got, seen_recv)
    for i in range(local):
        key_work[i] = seen_got[:, 0].reshape(patches * span, HEAD_DIM)
        value_work[i] = seen_got[:, 1].reshape(patches * span, HEAD_DIM)
    wait_bytes(fresh_got, fresh_recv)

    scale_qk = 1.0 / math.sqrt(HEAD_DIM)

    def attended_args(slot, patch, i):
        to = lax.rem(p + 1 + i, patches)
        return (attended_out.at[slot], attended_got.at[patch, my_head],
                attended_send.at[slot, to], attended_recv.at[patch], (to, u), here)

    def attend(slot):
        index = lax.rem(slot + u, local)
        patch = my_rank * local + index
        query = fresh_got[index, :, 0].reshape(span, HEAD_DIM)
        own = pl.ds(pl.multiple_of(patch * span, span), span)
        key_work[slot, own] = fresh_got[index, :, 1].reshape(span, HEAD_DIM)
        value_work[slot, own] = fresh_got[index, :, 2].reshape(span, HEAD_DIM)
        scores = lax.dot_general(
            query, key_work[slot], (((1,), (1,)), ((), ())), preferred_element_type=jnp.float32
        ) * scale_qk
        top = jnp.max(scores, axis=1, keepdims=True)
        weights = jnp.exp(scores - top)
        total = jnp.sum(weights, axis=1, keepdims=True)
        mixed = jnp.dot(
            weights.astype(jnp.bfloat16), value_work[slot], preferred_element_type=jnp.float32
        )
        attended_out[slot] = (mixed / total).astype(jnp.bfloat16)

        def start(i, carry):
            send(*attended_args(slot, patch, i))
            return carry

        lax.fori_loop(0, patches, start, 0)

    def terms_args(patch, i):
        to = lax.rem(u + 1 + i, groups)
        return (terms_out.at[patch, to], terms_got.at[u, p],
                terms_send.at[patch, to], terms_recv, (patch, to), here)

    def project(slot):
        index = lax.rem(slot + u, local)
        for r in range(ranks):
            patch = r * local + index
            wait_bytes(attended_got.at[patch], attended_recv.at[patch])
            gathered = jnp.concatenate([attended_got[patch, l] for l in range(local)], axis=1)
            terms = jnp.dot(gathered, weight_in[...], preferred_element_type=jnp.float32)
            terms_out[patch] = terms.astype(jnp.bfloat16).reshape(groups, rows, terms.shape[1])

            def start(i, carry):
                send(*terms_args(patch, i))
                return carry

            lax.fori_loop(0, groups, start, 0)

    for slot in range(local):
        attend(slot)
    loads[7].wait()
    for slot in range(local):
        project(slot)

    def end_fresh(i, carry):
        finish_send(*fresh_args(i))
        return carry

    def end_seen(i, carry):
        finish_send(*seen_args(i))
        return carry

    lax.fori_loop(0, heads, end_fresh, 0)
    lax.fori_loop(0, patches, end_seen, 0)
    for slot in range(local):
        patch = my_rank * local + lax.rem(slot + u, local)

        def end(i, carry):
            finish_send(*attended_args(slot, patch, i))
            return carry

        lax.fori_loop(0, patches, end, 0)

    def end_terms(i, carry):
        finish_send(*terms_args(i // groups, lax.rem(i, groups)))
        return carry

    wait_bytes(terms_got, terms_recv)
    columns = weight.shape[1]
    for q in range(patches):
        total = terms_got[0, q].astype(jnp.float32)
        for g in range(1, groups):
            total = total + terms_got[g, q].astype(jnp.float32)
        out[:, q * columns:(q + 1) * columns] = total.astype(jnp.bfloat16)
    lax.fori_loop(0, patches * groups, end_terms, 0)


def solution(mesh):
    patches, groups = mesh.shape["patch"], mesh.shape["ulysses"]

    def on_device(
        fresh_queries, fresh_keys, fresh_values, outdated_keys, stale_values,
        key_codes, value_codes, key_code_scales, value_scales, out_weight,
    ):
        rows, width = fresh_queries.shape
        span = rows * groups
        heads = width // HEAD_DIM
        local = heads // groups
        depth, columns = out_weight.shape
        bf16, f32 = jnp.bfloat16, jnp.float32
        vmem = pl.BlockSpec(memory_space=pltpu.VMEM)
        hbm = pl.BlockSpec(memory_space=pltpu.HBM)
        dma = pltpu.SemaphoreType.DMA
        return pl.pallas_call(
            functools.partial(kernel, patches, groups),
            out_shape=jax.ShapeDtypeStruct((rows, patches * columns), bf16),
            in_specs=[vmem] * 2 + [hbm] * 8,
            out_specs=vmem,
            scratch_shapes=[
                pltpu.VMEM((3, rows, width), bf16),
                pltpu.VMEM((2, span, depth), bf16),
                pltpu.VMEM((2, span, depth), jnp.int32),
                pltpu.VMEM((depth, columns), bf16),
                pltpu.VMEM((heads, 3, rows, HEAD_DIM), bf16),
                pltpu.VMEM((local, groups, 3, rows, HEAD_DIM), bf16),
                pltpu.VMEM((local, 2, span, HEAD_DIM), bf16),
                pltpu.VMEM((patches, 2, span, HEAD_DIM), bf16),
                pltpu.VMEM((local, patches * span, HEAD_DIM), bf16),
                pltpu.VMEM((local, patches * span, HEAD_DIM), bf16),
                pltpu.VMEM((local, span, HEAD_DIM), bf16),
                pltpu.VMEM((patches, local, span, HEAD_DIM), bf16),
                pltpu.VMEM((patches, groups, rows, columns), bf16),
                pltpu.VMEM((groups, patches, rows, columns), bf16),
                dma((8,)), dma((heads,)), dma, dma((patches,)), dma,
                dma((local, patches)), dma((patches,)), dma((patches, groups)), dma,
            ],
            compiler_params=pltpu.CompilerParams(
                collective_id=0, has_side_effects=True, vmem_limit_bytes=60 * 1024 * 1024
            ),
        )(
            key_code_scales.T, value_scales.T, fresh_queries, fresh_keys, fresh_values,
            outdated_keys, stale_values, key_codes, value_codes, out_weight,
        )

    return jax.shard_map(
        on_device,
        mesh=mesh,
        in_specs=(
            P(("patch", "ulysses"), None),
            P(("patch", "ulysses"), None),
            P(("patch", "ulysses"), None),
            P(None, "ulysses"),
            P(None, "ulysses"),
            P("patch", "ulysses"),
            P("patch", "ulysses"),
            P("patch", "ulysses"),
            P("patch", "ulysses"),
            P("ulysses", "patch"),
        ),
        out_specs=P(("patch", "ulysses"), None),
        check_vma=False,
    )
```

```python
import functools
import math

import jax
import jax.numpy as jnp
from jax import lax
from jax.experimental import pallas as pl
from jax.experimental.pallas import tpu as pltpu
from jax.sharding import PartitionSpec as P

HEAD_DIM = 128
BLOCK = 8
MESH = pl.DeviceIdType.MESH


def send(src, dst, send_sem, recv_sem, target, here):
    same = jnp.logical_and(target[0] == here[0], target[1] == here[1])

    @pl.when(same)
    def _():
        pltpu.make_async_copy(src, dst, recv_sem).start()

    @pl.when(jnp.logical_not(same))
    def _():
        pltpu.make_async_remote_copy(
            src, dst, send_sem, recv_sem, device_id=target, device_id_type=MESH
        ).start()


def finish_send(src, dst, send_sem, recv_sem, target, here):
    same = jnp.logical_and(target[0] == here[0], target[1] == here[1])

    @pl.when(jnp.logical_not(same))
    def _():
        pltpu.make_async_remote_copy(
            src, dst, send_sem, recv_sem, device_id=target, device_id_type=MESH
        ).wait_send()


def wait_bytes(buffer, sem):
    pltpu.make_async_copy(buffer, buffer, sem).wait()


def kernel(
    patches, groups,
    key_scales, value_scales,
    fresh_q, fresh_k, fresh_v, old_k, old_v, codes_k, codes_v, weight,
    out,
    fresh_in, old_in, codes_in, weight_got,
    fresh_out, fresh_got, seen_out, seen_got, key_work, value_work,
    attended_out, attended_got, terms_out, terms_got,
    load_sem, weight_send, weight_recv, fresh_send, fresh_recv,
    seen_send, seen_recv, pass_send, pass_recv,
    attended_send, attended_recv, terms_send, terms_recv,
):
    p = lax.axis_index("patch")
    u = lax.axis_index("ulysses")
    here = (p, u)
    rows = fresh_q.shape[0]
    span = rows * groups
    heads = fresh_q.shape[1] // HEAD_DIM
    local = heads // groups
    ranks = patches // local
    my_head = p // ranks
    my_rank = lax.rem(p, ranks)

    loads = [
        pltpu.make_async_copy(source, fresh_in.at[i], load_sem.at[i])
        for i, source in enumerate((fresh_q, fresh_k, fresh_v))
    ]
    first = pl.multiple_of(p * span, span)
    loads.append(pltpu.make_async_copy(old_k.at[pl.ds(first, span)], old_in.at[0], load_sem.at[3]))
    loads.append(pltpu.make_async_copy(old_v.at[pl.ds(first, span)], old_in.at[1], load_sem.at[4]))
    loads.append(pltpu.make_async_copy(codes_k, codes_in.at[0], load_sem.at[5]))
    loads.append(pltpu.make_async_copy(codes_v, codes_in.at[1], load_sem.at[6]))
    loads.append(pltpu.make_async_copy(weight, weight_got.at[my_rank], load_sem.at[7]))
    for load in loads:
        load.start()

    barrier = pltpu.get_barrier_semaphore()
    devices = patches * groups

    def greet(i, carry):
        to_p, to_u = i // groups, lax.rem(i, groups)

        @pl.when(jnp.logical_not(jnp.logical_and(to_p == p, to_u == u)))
        def _():
            pl.semaphore_signal(barrier, inc=1, device_id=(to_p, to_u), device_id_type=MESH)

        return carry

    lax.fori_loop(0, devices, greet, 0)

    for load in loads[:3]:
        load.wait()
    for h in range(heads):
        for i in range(3):
            fresh_out[h, i] = fresh_in[i, :, h * HEAD_DIM:(h + 1) * HEAD_DIM]
    for load in loads[3:7]:
        load.wait()
    block_of = lax.broadcasted_iota(jnp.int32, (span, span // BLOCK), 0) // BLOCK
    pick = (block_of == lax.broadcasted_iota(jnp.int32, (span, span // BLOCK), 1)).astype(jnp.float32)
    for i, scales in enumerate((key_scales, value_scales)):
        wide = lax.dot_general(
            pick, scales[...].astype(jnp.float32), (((1,), (1,)), ((), ())),
            preferred_element_type=jnp.float32,
        )
        for l in range(local):
            cols = slice(l * HEAD_DIM, (l + 1) * HEAD_DIM)
            seen_out[l, i] = (
                old_in[i, :, cols].astype(jnp.float32)
                + wide[:, l:l + 1] * codes_in[i, :, cols].astype(jnp.float32)
            ).astype(jnp.bfloat16)

    pl.semaphore_wait(barrier, devices - 1)

    def fresh_args(i):
        h = lax.rem(u * local + local + i, heads)
        target = (lax.rem(h, local) * ranks + p // local, h // local)
        return (fresh_out.at[h], fresh_got.at[lax.rem(p, local), u],
                fresh_send.at[h], fresh_recv, target, here)

    def seen_args(i):
        m = lax.rem(my_head + i, local)
        return (seen_out.at[m], seen_got.at[my_rank, my_head], seen_send.at[m],
                seen_recv.at[my_head], (m * ranks + my_rank, u), here)

    def pass_args(m, i):
        to = lax.rem(my_rank + 1 + i, ranks)
        block = seen_got.at[my_rank, m]
        return (block, block, pass_send.at[m, to], pass_recv.at[my_rank],
                (my_head * ranks + to, u), here)

    def weight_args(i):
        to = lax.rem(my_rank + 1 + i, ranks)
        return (weight, weight_got.at[my_rank], weight_send.at[to], weight_recv.at[my_rank],
                (my_head * ranks + to, u), here)

    def start_fresh(i, carry):
        send(*fresh_args(i))
        return carry

    def start_weight(i, carry):
        send(*weight_args(i))
        return carry

    for i in range(local):
        send(*seen_args(i))
    lax.fori_loop(0, heads, start_fresh, 0)
    for i in range(local):
        m = lax.rem(my_head + local - i, local)
        wait_bytes(seen_got.at[my_rank, m], seen_recv.at[m])

        def start_pass(i, carry):
            send(*pass_args(m, i))
            return carry

        lax.fori_loop(0, ranks - 1, start_pass, 0)
    lax.fori_loop(0, ranks - 1, start_weight, 0)

    def wait_pass(i, carry):
        source = lax.rem(my_rank + 1 + i, ranks)
        wait_bytes(seen_got.at[source], pass_recv.at[source])
        return carry

    lax.fori_loop(0, ranks - 1, wait_pass, 0)
    for i in range(local):
        key_work[i] = seen_got[:, :, 0].reshape(patches * span, HEAD_DIM)
        value_work[i] = seen_got[:, :, 1].reshape(patches * span, HEAD_DIM)
    wait_bytes(fresh_got, fresh_recv)

    scale_qk = 1.0 / math.sqrt(HEAD_DIM)

    def attended_args(slot, index, i):
        m = lax.rem(my_head + 1 + i, local)
        return (attended_out.at[slot], attended_got.at[index, my_head],
                attended_send.at[slot, m], attended_recv.at[index], (m * ranks + my_rank, u), here)

    def attend(slot):
        index = lax.rem(slot + u, local)
        patch = my_rank * local + index
        query = fresh_got[index, :, 0].reshape(span, HEAD_DIM)
        place = lax.rem(patch, ranks) * local + patch // ranks
        own = pl.ds(pl.multiple_of(place * span, span), span)
        key_work[slot, own] = fresh_got[index, :, 1].reshape(span, HEAD_DIM)
        value_work[slot, own] = fresh_got[index, :, 2].reshape(span, HEAD_DIM)
        scores = lax.dot_general(
            query, key_work[slot], (((1,), (1,)), ((), ())), preferred_element_type=jnp.float32
        ) * scale_qk
        top = jnp.max(scores, axis=1, keepdims=True)
        weights = jnp.exp(scores - top)
        total = jnp.sum(weights, axis=1, keepdims=True)
        mixed = jnp.dot(
            weights.astype(jnp.bfloat16), value_work[slot], preferred_element_type=jnp.float32
        )
        attended_out[slot] = (mixed / total).astype(jnp.bfloat16)

        def start(i, carry):
            send(*attended_args(slot, index, i))
            return carry

        lax.fori_loop(0, local, start, 0)

    def terms_args(index, i):
        to = lax.rem(u + 1 + i, groups)
        return (terms_out.at[index, to], terms_got.at[u, my_head], terms_send.at[index, to],
                terms_recv, (my_rank * local + index, to), here)

    def project(slot):
        index = lax.rem(slot + u, local)
        wait_bytes(attended_got.at[index], attended_recv.at[index])
        gathered = jnp.concatenate([attended_got[index, l] for l in range(local)], axis=1)
        for r in range(ranks):
            terms = jnp.dot(gathered, weight_got[r], preferred_element_type=jnp.float32)
            terms_out[index, :, r] = terms.astype(jnp.bfloat16).reshape(groups, rows, terms.shape[1])

        def start(i, carry):
            send(*terms_args(index, i))
            return carry

        lax.fori_loop(0, groups, start, 0)

    for slot in range(local):
        attend(slot)
    loads[7].wait()

    def wait_weight(i, carry):
        source = lax.rem(my_rank + 1 + i, ranks)
        wait_bytes(weight_got.at[source], weight_recv.at[source])
        return carry

    lax.fori_loop(0, ranks - 1, wait_weight, 0)
    for slot in range(local):
        project(slot)

    wait_bytes(terms_got, terms_recv)
    columns = weight.shape[1]
    for q in range(patches):
        total = terms_got[0, q // ranks, q % ranks].astype(jnp.float32)
        for g in range(1, groups):
            total = total + terms_got[g, q // ranks, q % ranks].astype(jnp.float32)
        out[:, q * columns:(q + 1) * columns] = total.astype(jnp.bfloat16)

    def end_fresh(i, carry):
        finish_send(*fresh_args(i))
        return carry

    def end_weight(i, carry):
        finish_send(*weight_args(i))
        return carry

    lax.fori_loop(0, heads, end_fresh, 0)
    lax.fori_loop(0, ranks - 1, end_weight, 0)
    for i in range(local):
        finish_send(*seen_args(i))

        def end_pass(k, carry):
            finish_send(*pass_args(i, k))
            return carry

        def end_attended(k, carry):
            finish_send(*attended_args(i, lax.rem(i + u, local), k))
            return carry

        def end_terms(k, carry):
            finish_send(*terms_args(i, k))
            return carry

        lax.fori_loop(0, ranks - 1, end_pass, 0)
        lax.fori_loop(0, local, end_attended, 0)
        lax.fori_loop(0, groups, end_terms, 0)


def solution(mesh):
    patches, groups = mesh.shape["patch"], mesh.shape["ulysses"]

    def on_device(
        fresh_queries, fresh_keys, fresh_values, outdated_keys, stale_values,
        key_codes, value_codes, key_code_scales, value_scales, out_weight,
    ):
        rows, width = fresh_queries.shape
        span = rows * groups
        heads = width // HEAD_DIM
        local = heads // groups
        ranks = patches // local
        depth, columns = out_weight.shape
        bf16, f32 = jnp.bfloat16, jnp.float32
        vmem = pl.BlockSpec(memory_space=pltpu.VMEM)
        hbm = pl.BlockSpec(memory_space=pltpu.HBM)
        dma = pltpu.SemaphoreType.DMA
        return pl.pallas_call(
            functools.partial(kernel, patches, groups),
            out_shape=jax.ShapeDtypeStruct((rows, patches * columns), bf16),
            in_specs=[vmem] * 2 + [hbm] * 8,
            out_specs=vmem,
            scratch_shapes=[
                pltpu.VMEM((3, rows, width), bf16),
                pltpu.VMEM((2, span, depth), bf16),
                pltpu.VMEM((2, span, depth), jnp.int32),
                pltpu.VMEM((ranks, depth, columns), bf16),
                pltpu.VMEM((heads, 3, rows, HEAD_DIM), bf16),
                pltpu.VMEM((local, groups, 3, rows, HEAD_DIM), bf16),
                pltpu.VMEM((local, 2, span, HEAD_DIM), bf16),
                pltpu.VMEM((ranks, local, 2, span, HEAD_DIM), bf16),
                pltpu.VMEM((local, patches * span, HEAD_DIM), bf16),
                pltpu.VMEM((local, patches * span, HEAD_DIM), bf16),
                pltpu.VMEM((local, span, HEAD_DIM), bf16),
                pltpu.VMEM((local, local, span, HEAD_DIM), bf16),
                pltpu.VMEM((local, groups, ranks, rows, columns), bf16),
                pltpu.VMEM((groups, local, ranks, rows, columns), bf16),
                dma((8,)), dma((ranks,)), dma((ranks,)), dma((heads,)), dma,
                dma((local,)), dma((local,)), dma((local, ranks)), dma((ranks,)),
                dma((local, local)), dma((local,)), dma((local, groups)), dma,
            ],
            compiler_params=pltpu.CompilerParams(
                collective_id=0, has_side_effects=True, vmem_limit_bytes=60 * 1024 * 1024
            ),
        )(
            key_code_scales.T, value_scales.T, fresh_queries, fresh_keys, fresh_values,
            outdated_keys, stale_values, key_codes, value_codes, out_weight,
        )

    return jax.shard_map(
        on_device,
        mesh=mesh,
        in_specs=(
            P(("patch", "ulysses"), None),
            P(("patch", "ulysses"), None),
            P(("patch", "ulysses"), None),
            P(None, "ulysses"),
            P(None, "ulysses"),
            P("patch", "ulysses"),
            P("patch", "ulysses"),
            P("patch", "ulysses"),
            P("patch", "ulysses"),
            P("ulysses", "patch"),
        ),
        out_specs=P(("patch", "ulysses"), None),
        check_vma=False,
    )
```

```python
import functools
import math

import jax
import jax.numpy as jnp
from jax import lax
from jax.experimental import pallas as pl
from jax.experimental.pallas import tpu as pltpu
from jax.sharding import PartitionSpec as P

HEAD_DIM = 128
BLOCK = 8
MESH = pl.DeviceIdType.MESH


def send(src, dst, send_sem, recv_sem, target, here):
    same = jnp.logical_and(target[0] == here[0], target[1] == here[1])

    @pl.when(same)
    def _():
        pltpu.make_async_copy(src, dst, recv_sem).start()

    @pl.when(jnp.logical_not(same))
    def _():
        pltpu.make_async_remote_copy(
            src, dst, send_sem, recv_sem, device_id=target, device_id_type=MESH
        ).start()


def finish_send(src, dst, send_sem, recv_sem, target, here):
    same = jnp.logical_and(target[0] == here[0], target[1] == here[1])

    @pl.when(jnp.logical_not(same))
    def _():
        pltpu.make_async_remote_copy(
            src, dst, send_sem, recv_sem, device_id=target, device_id_type=MESH
        ).wait_send()


def wait_bytes(buffer, sem):
    pltpu.make_async_copy(buffer, buffer, sem).wait()


def kernel(
    patches, groups,
    key_scales, value_scales,
    fresh_q, fresh_k, fresh_v, old_k, old_v, codes_k, codes_v, weight,
    terms_got,
    fresh_in, old_in, codes_in, weight_got,
    fresh_out, fresh_got, seen_out, seen_got, key_work, value_work,
    attended_out, attended_got, terms_out,
    load_sem, weight_send, weight_recv, fresh_send, fresh_recv,
    seen_send, seen_recv, pass_send, pass_recv,
    attended_send, attended_recv, terms_send, terms_recv,
):
    p = lax.axis_index("patch")
    u = lax.axis_index("ulysses")
    here = (p, u)
    rows = fresh_q.shape[0]
    span = rows * groups
    heads = fresh_q.shape[1] // HEAD_DIM
    local = heads // groups
    ranks = patches // local
    my_head = p // ranks
    my_rank = lax.rem(p, ranks)

    barrier = pltpu.get_barrier_semaphore()
    devices = patches * groups

    def greet(i, carry):
        to_p, to_u = i // groups, lax.rem(i, groups)

        @pl.when(jnp.logical_not(jnp.logical_and(to_p == p, to_u == u)))
        def _():
            pl.semaphore_signal(barrier, inc=1, device_id=(to_p, to_u), device_id_type=MESH)

        return carry

    lax.fori_loop(0, devices, greet, 0)

    loads = [
        pltpu.make_async_copy(source, fresh_in.at[i], load_sem.at[i])
        for i, source in enumerate((fresh_q, fresh_k, fresh_v))
    ]
    first = pl.multiple_of(p * span, span)
    loads.append(pltpu.make_async_copy(old_k.at[pl.ds(first, span)], old_in.at[0], load_sem.at[3]))
    loads.append(pltpu.make_async_copy(old_v.at[pl.ds(first, span)], old_in.at[1], load_sem.at[4]))
    loads.append(pltpu.make_async_copy(codes_k, codes_in.at[0], load_sem.at[5]))
    loads.append(pltpu.make_async_copy(codes_v, codes_in.at[1], load_sem.at[6]))
    loads.append(pltpu.make_async_copy(weight, weight_got.at[my_rank], load_sem.at[7]))
    for load in loads:
        load.start()

    for load in loads[:3]:
        load.wait()
    for h in range(heads):
        for i in range(3):
            fresh_out[h, i] = fresh_in[i, :, h * HEAD_DIM:(h + 1) * HEAD_DIM]
    for load in loads[3:7]:
        load.wait()
    block_of = lax.broadcasted_iota(jnp.int32, (span, span // BLOCK), 0) // BLOCK
    pick = (block_of == lax.broadcasted_iota(jnp.int32, (span, span // BLOCK), 1)).astype(jnp.float32)
    for i, scales in enumerate((key_scales, value_scales)):
        wide = lax.dot_general(
            pick, scales[...].astype(jnp.float32), (((1,), (1,)), ((), ())),
            preferred_element_type=jnp.float32,
        )
        for l in range(local):
            cols = slice(l * HEAD_DIM, (l + 1) * HEAD_DIM)
            seen_out[l, i] = (
                old_in[i, :, cols].astype(jnp.float32)
                + wide[:, l:l + 1] * codes_in[i, :, cols].astype(jnp.float32)
            ).astype(jnp.bfloat16)

    pl.semaphore_wait(barrier, devices - 1)

    def fresh_args(i):
        h = lax.rem(u * local + local + i, heads)
        target = (lax.rem(h, local) * ranks + p // local, h // local)
        return (fresh_out.at[h], fresh_got.at[lax.rem(p, local), u],
                fresh_send.at[h], fresh_recv, target, here)

    def seen_args(i):
        m = lax.rem(my_head + i, local)
        return (seen_out.at[m], seen_got.at[my_rank, my_head], seen_send.at[m],
                seen_recv.at[my_head], (m * ranks + my_rank, u), here)

    def pass_args(m, i):
        to = lax.rem(my_rank + 1 + i, ranks)
        block = seen_got.at[my_rank, m]
        return (block, block, pass_send.at[m, to], pass_recv.at[my_rank],
                (my_head * ranks + to, u), here)

    def weight_args(i):
        to = lax.rem(my_rank + 1 + i, ranks)
        return (weight, weight_got.at[my_rank], weight_send.at[to], weight_recv.at[my_rank],
                (my_head * ranks + to, u), here)

    def start_fresh(i, carry):
        send(*fresh_args(i))
        return carry

    def start_weight(i, carry):
        send(*weight_args(i))
        return carry

    for i in range(local):
        send(*seen_args(i))
    lax.fori_loop(0, heads, start_fresh, 0)
    for i in range(local):
        m = lax.rem(my_head + local - i, local)
        wait_bytes(seen_got.at[my_rank, m], seen_recv.at[m])

        def start_pass(i, carry):
            send(*pass_args(m, i))
            return carry

        lax.fori_loop(0, ranks - 1, start_pass, 0)
    lax.fori_loop(0, ranks - 1, start_weight, 0)

    def wait_pass(i, carry):
        source = lax.rem(my_rank + 1 + i, ranks)
        wait_bytes(seen_got.at[source], pass_recv.at[source])
        return carry

    lax.fori_loop(0, ranks - 1, wait_pass, 0)
    for i in range(local):
        key_work[i] = seen_got[:, :, 0].reshape(patches * span, HEAD_DIM)
        value_work[i] = seen_got[:, :, 1].reshape(patches * span, HEAD_DIM)
    wait_bytes(fresh_got, fresh_recv)

    scale_qk = 1.0 / math.sqrt(HEAD_DIM)

    def attended_args(slot, index, i):
        m = lax.rem(my_head + 1 + i, local)
        return (attended_out.at[slot], attended_got.at[index, my_head],
                attended_send.at[slot, m], attended_recv.at[index], (m * ranks + my_rank, u), here)

    def attend(slot):
        index = lax.rem(slot + u, local)
        patch = my_rank * local + index
        query = fresh_got[index, :, 0].reshape(span, HEAD_DIM)
        place = lax.rem(patch, ranks) * local + patch // ranks
        own = pl.ds(pl.multiple_of(place * span, span), span)
        key_work[slot, own] = fresh_got[index, :, 1].reshape(span, HEAD_DIM)
        value_work[slot, own] = fresh_got[index, :, 2].reshape(span, HEAD_DIM)
        scores = lax.dot_general(
            query, key_work[slot], (((1,), (1,)), ((), ())), preferred_element_type=jnp.float32
        ) * scale_qk
        top = jnp.max(scores, axis=1, keepdims=True)
        weights = jnp.exp(scores - top)
        total = jnp.sum(weights, axis=1, keepdims=True)
        mixed = jnp.dot(
            weights.astype(jnp.bfloat16), value_work[slot], preferred_element_type=jnp.float32
        )
        attended_out[slot] = (mixed / total).astype(jnp.bfloat16)

        def start(i, carry):
            send(*attended_args(slot, index, i))
            return carry

        lax.fori_loop(0, local, start, 0)

    columns = weight.shape[1]
    width = ranks * columns
    place = 0 if local == 1 else pl.multiple_of(my_head * width, width)

    def terms_args(index, i):
        to = lax.rem(u + 1 + i, groups)
        return (terms_out.at[index, to], terms_got.at[u, :, pl.ds(place, width)], terms_send.at[index, to],
                terms_recv, (my_rank * local + index, to), here)

    def project(slot):
        index = lax.rem(slot + u, local)
        wait_bytes(attended_got.at[index], attended_recv.at[index])
        gathered = jnp.concatenate([attended_got[index, l] for l in range(local)], axis=1)
        for r in range(ranks):
            terms = jnp.dot(gathered, weight_got[r], preferred_element_type=jnp.float32)
            terms_out[index, :, :, r * columns:(r + 1) * columns] = terms.astype(jnp.bfloat16).reshape(
                groups, rows, columns
            )

        def start(i, carry):
            send(*terms_args(index, i))
            return carry

        lax.fori_loop(0, groups, start, 0)

    for slot in range(local):
        attend(slot)
    loads[7].wait()

    def wait_weight(i, carry):
        source = lax.rem(my_rank + 1 + i, ranks)
        wait_bytes(weight_got.at[source], weight_recv.at[source])
        return carry

    lax.fori_loop(0, ranks - 1, wait_weight, 0)
    for slot in range(local):
        project(slot)

    wait_bytes(terms_got, terms_recv)

    def end_fresh(i, carry):
        finish_send(*fresh_args(i))
        return carry

    def end_weight(i, carry):
        finish_send(*weight_args(i))
        return carry

    lax.fori_loop(0, heads, end_fresh, 0)
    lax.fori_loop(0, ranks - 1, end_weight, 0)
    for i in range(local):
        finish_send(*seen_args(i))

        def end_pass(k, carry):
            finish_send(*pass_args(i, k))
            return carry

        def end_attended(k, carry):
            finish_send(*attended_args(i, lax.rem(i + u, local), k))
            return carry

        def end_terms(k, carry):
            finish_send(*terms_args(i, k))
            return carry

        lax.fori_loop(0, ranks - 1, end_pass, 0)
        lax.fori_loop(0, local, end_attended, 0)
        lax.fori_loop(0, groups, end_terms, 0)


def solution(mesh):
    patches, groups = mesh.shape["patch"], mesh.shape["ulysses"]

    def on_device(
        fresh_queries, fresh_keys, fresh_values, outdated_keys, stale_values,
        key_codes, value_codes, key_code_scales, value_scales, out_weight,
    ):
        rows, width = fresh_queries.shape
        span = rows * groups
        heads = width // HEAD_DIM
        local = heads // groups
        ranks = patches // local
        depth, columns = out_weight.shape
        bf16, f32 = jnp.bfloat16, jnp.float32
        vmem = pl.BlockSpec(memory_space=pltpu.VMEM)
        hbm = pl.BlockSpec(memory_space=pltpu.HBM)
        dma = pltpu.SemaphoreType.DMA
        terms = pl.pallas_call(
            functools.partial(kernel, patches, groups),
            out_shape=jax.ShapeDtypeStruct((groups, rows, patches * columns), bf16),
            in_specs=[vmem] * 2 + [hbm] * 8,
            out_specs=hbm,
            scratch_shapes=[
                pltpu.VMEM((3, rows, width), bf16),
                pltpu.VMEM((2, span, depth), bf16),
                pltpu.VMEM((2, span, depth), jnp.int32),
                pltpu.VMEM((ranks, depth, columns), bf16),
                pltpu.VMEM((heads, 3, rows, HEAD_DIM), bf16),
                pltpu.VMEM((local, groups, 3, rows, HEAD_DIM), bf16),
                pltpu.VMEM((local, 2, span, HEAD_DIM), bf16),
                pltpu.VMEM((ranks, local, 2, span, HEAD_DIM), bf16),
                pltpu.VMEM((local, patches * span, HEAD_DIM), bf16),
                pltpu.VMEM((local, patches * span, HEAD_DIM), bf16),
                pltpu.VMEM((local, span, HEAD_DIM), bf16),
                pltpu.VMEM((local, local, span, HEAD_DIM), bf16),
                pltpu.VMEM((local, groups, rows, ranks * columns), bf16),
                dma((8,)), dma((ranks,)), dma((ranks,)), dma((heads,)), dma,
                dma((local,)), dma((local,)), dma((local, ranks)), dma((ranks,)),
                dma((local, local)), dma((local,)), dma((local, groups)), dma,
            ],
            compiler_params=pltpu.CompilerParams(
                collective_id=0, has_side_effects=True, vmem_limit_bytes=60 * 1024 * 1024
            ),
        )(
            key_code_scales.T, value_scales.T, fresh_queries, fresh_keys, fresh_values,
            outdated_keys, stale_values, key_codes, value_codes, out_weight,
        )
        total = terms[0].astype(f32)
        for g in range(1, groups):
            total = total + terms[g].astype(f32)
        return total.astype(bf16)

    return jax.shard_map(
        on_device,
        mesh=mesh,
        in_specs=(
            P(("patch", "ulysses"), None),
            P(("patch", "ulysses"), None),
            P(("patch", "ulysses"), None),
            P(None, "ulysses"),
            P(None, "ulysses"),
            P("patch", "ulysses"),
            P("patch", "ulysses"),
            P("patch", "ulysses"),
            P("patch", "ulysses"),
            P("ulysses", "patch"),
        ),
        out_specs=P(("patch", "ulysses"), None),
        check_vma=False,
    )
```

```python
import functools
import math

import jax
import jax.numpy as jnp
from jax import lax
from jax.experimental import pallas as pl
from jax.experimental.pallas import tpu as pltpu
from jax.sharding import PartitionSpec as P

HEAD_DIM = 128
BLOCK = 8
MESH = pl.DeviceIdType.MESH


def send(src, dst, send_sem, recv_sem, target, here):
    same = jnp.logical_and(target[0] == here[0], target[1] == here[1])

    @pl.when(same)
    def _():
        pltpu.make_async_copy(src, dst, recv_sem).start()

    @pl.when(jnp.logical_not(same))
    def _():
        pltpu.make_async_remote_copy(
            src, dst, send_sem, recv_sem, device_id=target, device_id_type=MESH
        ).start()


def finish_send(src, dst, send_sem, recv_sem, target, here):
    same = jnp.logical_and(target[0] == here[0], target[1] == here[1])

    @pl.when(jnp.logical_not(same))
    def _():
        pltpu.make_async_remote_copy(
            src, dst, send_sem, recv_sem, device_id=target, device_id_type=MESH
        ).wait_send()


def wait_bytes(buffer, sem):
    pltpu.make_async_copy(buffer, buffer, sem).wait()


def kernel(
    patches, groups,
    key_scales, value_scales,
    fresh_q, fresh_k, fresh_v, old_k, old_v, codes_k, codes_v, weight,
    terms_got,
    fresh_in, old_in, codes_in, weight_got,
    fresh_out, fresh_got, seen_out, seen_got, key_work, value_work,
    attended_out, attended_got, terms_out,
    load_sem, weight_send, weight_recv, fresh_send, fresh_recv,
    seen_send, seen_recv, pass_send, pass_recv,
    attended_send, attended_recv, terms_send, terms_recv,
):
    p = lax.axis_index("patch")
    u = lax.axis_index("ulysses")
    here = (p, u)
    rows = fresh_q.shape[0]
    span = rows * groups
    heads = fresh_q.shape[1] // HEAD_DIM
    local = heads // groups
    ranks = patches // local
    my_head = p // ranks
    my_rank = lax.rem(p, ranks)

    barrier = pltpu.get_barrier_semaphore()
    devices = patches * groups

    def greet(i, carry):
        to_p, to_u = i // groups, lax.rem(i, groups)

        @pl.when(jnp.logical_not(jnp.logical_and(to_p == p, to_u == u)))
        def _():
            pl.semaphore_signal(barrier, inc=1, device_id=(to_p, to_u), device_id_type=MESH)

        return carry

    lax.fori_loop(0, devices, greet, 0)

    loads = [
        pltpu.make_async_copy(source, fresh_in.at[i], load_sem.at[i])
        for i, source in enumerate((fresh_q, fresh_k, fresh_v))
    ]
    first = pl.multiple_of(p * span, span)
    loads.append(pltpu.make_async_copy(old_k.at[pl.ds(first, span)], old_in.at[0], load_sem.at[3]))
    loads.append(pltpu.make_async_copy(old_v.at[pl.ds(first, span)], old_in.at[1], load_sem.at[4]))
    loads.append(pltpu.make_async_copy(codes_k, codes_in.at[0], load_sem.at[5]))
    loads.append(pltpu.make_async_copy(codes_v, codes_in.at[1], load_sem.at[6]))
    loads.append(pltpu.make_async_copy(weight, weight_got.at[my_rank], load_sem.at[7]))
    for load in loads:
        load.start()

    for load in loads[:3]:
        load.wait()
    for h in range(heads):
        for i in range(3):
            fresh_out[h, i] = fresh_in[i, :, h * HEAD_DIM:(h + 1) * HEAD_DIM]
    for load in loads[3:7]:
        load.wait()
    block_of = lax.broadcasted_iota(jnp.int32, (span, span // BLOCK), 0) // BLOCK
    pick = (block_of == lax.broadcasted_iota(jnp.int32, (span, span // BLOCK), 1)).astype(jnp.float32)
    for i, scales in enumerate((key_scales, value_scales)):
        wide = lax.dot_general(
            pick, scales[...].astype(jnp.float32), (((1,), (1,)), ((), ())),
            preferred_element_type=jnp.float32,
        )
        for l in range(local):
            cols = slice(l * HEAD_DIM, (l + 1) * HEAD_DIM)
            seen_out[l, i] = (
                old_in[i, :, cols].astype(jnp.float32)
                + wide[:, l:l + 1] * codes_in[i, :, cols].astype(jnp.float32)
            ).astype(jnp.bfloat16)

    pl.semaphore_wait(barrier, devices - 1)

    def fresh_args(i):
        h = lax.rem(u * local + local + i, heads)
        target = (lax.rem(h, local) * ranks + p // local, h // local)
        return (fresh_out.at[h], fresh_got.at[lax.rem(p, local), u],
                fresh_send.at[h], fresh_recv, target, here)

    def seen_args(i):
        m = lax.rem(my_head + i, local)
        return (seen_out.at[m], seen_got.at[my_rank, my_head], seen_send.at[m],
                seen_recv.at[my_head], (m * ranks + my_rank, u), here)

    def pass_args(m, i):
        to = lax.rem(my_rank + 1 + i, ranks)
        block = seen_got.at[my_rank, m]
        return (block, block, pass_send.at[m, to], pass_recv.at[my_rank],
                (my_head * ranks + to, u), here)

    def weight_args(i):
        to = lax.rem(my_rank + 1 + i, ranks)
        return (weight, weight_got.at[my_rank], weight_send.at[to], weight_recv.at[my_rank],
                (my_head * ranks + to, u), here)

    def start_fresh(i, carry):
        send(*fresh_args(i))
        return carry

    def start_weight(i, carry):
        send(*weight_args(i))
        return carry

    for i in range(local):
        send(*seen_args(i))
    lax.fori_loop(0, heads, start_fresh, 0)
    for i in range(local):
        m = lax.rem(my_head + local - i, local)
        wait_bytes(seen_got.at[my_rank, m], seen_recv.at[m])

        def start_pass(i, carry):
            send(*pass_args(m, i))
            return carry

        lax.fori_loop(0, ranks - 1, start_pass, 0)
    lax.fori_loop(0, ranks - 1, start_weight, 0)

    def wait_pass(i, carry):
        source = lax.rem(my_rank + 1 + i, ranks)
        wait_bytes(seen_got.at[source], pass_recv.at[source])
        return carry

    lax.fori_loop(0, ranks - 1, wait_pass, 0)
    for i in range(local):
        key_work[i] = seen_got[:, :, 0].reshape(patches * span, HEAD_DIM)
        value_work[i] = seen_got[:, :, 1].reshape(patches * span, HEAD_DIM)
    wait_bytes(fresh_got, fresh_recv)

    scale_qk = 1.0 / math.sqrt(HEAD_DIM)

    def attended_args(slot, index, i):
        m = lax.rem(my_head + 1 + i, local)
        return (attended_out.at[slot], attended_got.at[index, my_head],
                attended_send.at[slot, m], attended_recv.at[index], (m * ranks + my_rank, u), here)

    def attend(slot):
        index = lax.rem(slot, local)
        patch = my_rank * local + index
        query = fresh_got[index, :, 0].reshape(span, HEAD_DIM)
        place = lax.rem(patch, ranks) * local + patch // ranks
        own = pl.ds(pl.multiple_of(place * span, span), span)
        key_work[slot, own] = fresh_got[index, :, 1].reshape(span, HEAD_DIM)
        value_work[slot, own] = fresh_got[index, :, 2].reshape(span, HEAD_DIM)
        scores = lax.dot_general(
            query, key_work[slot], (((1,), (1,)), ((), ())), preferred_element_type=jnp.float32
        ) * scale_qk
        top = jnp.max(scores, axis=1, keepdims=True)
        weights = jnp.exp(scores - top)
        total = jnp.sum(weights, axis=1, keepdims=True)
        mixed = jnp.dot(
            weights.astype(jnp.bfloat16), value_work[slot], preferred_element_type=jnp.float32
        )
        attended_out[slot] = (mixed / total).astype(jnp.bfloat16)

        def start(i, carry):
            send(*attended_args(slot, index, i))
            return carry

        lax.fori_loop(0, local, start, 0)

    columns = weight.shape[1]
    width = ranks * columns
    place = 0 if local == 1 else pl.multiple_of(my_head * width, width)

    def terms_args(index, i):
        to = lax.rem(u + 1 + i, groups)
        return (terms_out.at[index, to], terms_got.at[u, :, pl.ds(place, width)], terms_send.at[index, to],
                terms_recv, (my_rank * local + index, to), here)

    def project(slot):
        index = lax.rem(slot, local)
        wait_bytes(attended_got.at[index], attended_recv.at[index])
        gathered = jnp.concatenate([attended_got[index, l] for l in range(local)], axis=1)
        for r in range(ranks):
            terms = jnp.dot(gathered, weight_got[r], preferred_element_type=jnp.float32)
            terms_out[index, :, :, r * columns:(r + 1) * columns] = terms.astype(jnp.bfloat16).reshape(
                groups, rows, columns
            )

        def start(i, carry):
            send(*terms_args(index, i))
            return carry

        lax.fori_loop(0, groups, start, 0)

    for slot in range(local):
        attend(slot)
    loads[7].wait()

    def wait_weight(i, carry):
        source = lax.rem(my_rank + 1 + i, ranks)
        wait_bytes(weight_got.at[source], weight_recv.at[source])
        return carry

    lax.fori_loop(0, ranks - 1, wait_weight, 0)
    for slot in range(local):
        project(slot)

    wait_bytes(terms_got, terms_recv)

    def end_fresh(i, carry):
        finish_send(*fresh_args(i))
        return carry

    def end_weight(i, carry):
        finish_send(*weight_args(i))
        return carry

    lax.fori_loop(0, heads, end_fresh, 0)
    lax.fori_loop(0, ranks - 1, end_weight, 0)
    for i in range(local):
        finish_send(*seen_args(i))

        def end_pass(k, carry):
            finish_send(*pass_args(i, k))
            return carry

        def end_attended(k, carry):
            finish_send(*attended_args(i, lax.rem(i, local), k))
            return carry

        def end_terms(k, carry):
            finish_send(*terms_args(i, k))
            return carry

        lax.fori_loop(0, ranks - 1, end_pass, 0)
        lax.fori_loop(0, local, end_attended, 0)
        lax.fori_loop(0, groups, end_terms, 0)


def solution(mesh):
    patches, groups = mesh.shape["patch"], mesh.shape["ulysses"]

    def on_device(
        fresh_queries, fresh_keys, fresh_values, outdated_keys, stale_values,
        key_codes, value_codes, key_code_scales, value_scales, out_weight,
    ):
        rows, width = fresh_queries.shape
        span = rows * groups
        heads = width // HEAD_DIM
        local = heads // groups
        ranks = patches // local
        depth, columns = out_weight.shape
        bf16, f32 = jnp.bfloat16, jnp.float32
        vmem = pl.BlockSpec(memory_space=pltpu.VMEM)
        hbm = pl.BlockSpec(memory_space=pltpu.HBM)
        dma = pltpu.SemaphoreType.DMA
        terms = pl.pallas_call(
            functools.partial(kernel, patches, groups),
            out_shape=jax.ShapeDtypeStruct((groups, rows, patches * columns), bf16),
            in_specs=[vmem] * 2 + [hbm] * 8,
            out_specs=hbm,
            scratch_shapes=[
                pltpu.VMEM((3, rows, width), bf16),
                pltpu.VMEM((2, span, depth), bf16),
                pltpu.VMEM((2, span, depth), jnp.int32),
                pltpu.VMEM((ranks, depth, columns), bf16),
                pltpu.VMEM((heads, 3, rows, HEAD_DIM), bf16),
                pltpu.VMEM((local, groups, 3, rows, HEAD_DIM), bf16),
                pltpu.VMEM((local, 2, span, HEAD_DIM), bf16),
                pltpu.VMEM((ranks, local, 2, span, HEAD_DIM), bf16),
                pltpu.VMEM((local, patches * span, HEAD_DIM), bf16),
                pltpu.VMEM((local, patches * span, HEAD_DIM), bf16),
                pltpu.VMEM((local, span, HEAD_DIM), bf16),
                pltpu.VMEM((local, local, span, HEAD_DIM), bf16),
                pltpu.VMEM((local, groups, rows, ranks * columns), bf16),
                dma((8,)), dma((ranks,)), dma((ranks,)), dma((heads,)), dma,
                dma((local,)), dma((local,)), dma((local, ranks)), dma((ranks,)),
                dma((local, local)), dma((local,)), dma((local, groups)), dma,
            ],
            compiler_params=pltpu.CompilerParams(
                collective_id=0, has_side_effects=True, vmem_limit_bytes=60 * 1024 * 1024
            ),
        )(
            key_code_scales.T, value_scales.T, fresh_queries, fresh_keys, fresh_values,
            outdated_keys, stale_values, key_codes, value_codes, out_weight,
        )
        total = terms[0].astype(f32)
        for g in range(1, groups):
            total = total + terms[g].astype(f32)
        return total.astype(bf16)

    return jax.shard_map(
        on_device,
        mesh=mesh,
        in_specs=(
            P(("patch", "ulysses"), None),
            P(("patch", "ulysses"), None),
            P(("patch", "ulysses"), None),
            P(None, "ulysses"),
            P(None, "ulysses"),
            P("patch", "ulysses"),
            P("patch", "ulysses"),
            P("patch", "ulysses"),
            P("patch", "ulysses"),
            P("ulysses", "patch"),
        ),
        out_specs=P(("patch", "ulysses"), None),
        check_vma=False,
    )
```
